32 devices in a mesh: src: 8 (over z, y), tgt: 4 (over x, core).
Axes of the slice: x: 2, y: 2, z: 4, core: 2. Of those that a mesh axis runs over, the one named last changes fastest.
Arguments:
- coefficients: float32 [256, 128, 512], P(('src', 'tgt')), may hold values from -6 to 6
- transfer: float32 [8, 256, 128, 256], P(None, ('src', 'tgt')), may hold values from -0.375 to 0.375
- local_bits: int32 [4], replicated, may hold values from 0 to 2
- relabel: int32 [1024], replicated, may hold values from 0 to 1023, each once
Outputs:
- result: float32 [256, 128, 512], P(('src', 'tgt'))
The draws below stay inside these ranges and needn't reach their ends.
Inputs may be any that keep to these rules, and one draw needn't show every extreme that they name: `local_bits`: each entry names a bit of a node's position among the 8 nodes of one device. `relabel`: a permutation of the 1024 rows of one device.
All inputs are finite; a program needn't handle non-finite values.
Results may differ from the reference program's by a relative error of at most 0.00007.
Values sent between devices are 32-bit elements; how exact they have to be, the bound alone decides.
No kernel may reach another device: no remote copies, remote signals or barrier semaphores. Data moves between devices by JAX's collectives and lax.ppermute only.
A program may use at most 64 MiB of HBM per device.

```python
import jax
import jax.numpy as jnp
from jax import lax

NODE_BITS = 3
NODES_DEV = 8
RANK = 128
RHS = 512
LOCAL_LEVELS = 4
LEVELS = 8
ROWS_DEV = 1024
NODES = 256
N_SRC = 8
N_TGT = 4


def place_ends(array, stream_key, least, top_value):
    dims = array.shape
    index_at = [jax.random.randint(jax.random.fold_in(stream_key, axis), (), 0, dims[axis]) for axis in range(len(dims))]
    array = array.at[tuple(index_at)].set(least)
    longest = dims.index(max(dims))
    index_at[longest] = (index_at[longest] + 1) % dims[longest]
    return array.at[tuple(index_at)].set(top_value)


def levels(key, extent, split, low, largest):
    factor_of, own = 1.0, jax.random.fold_in(key, 6)
    for position, parts in split:
        draws = jnp.exp(jax.random.uniform(jax.random.fold_in(own, position), (parts,), jnp.float32, low / len(split), largest / len(split)))
        factor_of = factor_of * jnp.repeat(draws, extent[position] // parts).reshape([-1 if axis == position else 1 for axis in range(len(extent))])
    return factor_of


def bell_draw(own_key, dims, deviation, limit, shards=(), kind=jnp.bfloat16):
    loudness = levels(own_key, dims, shards, -0.22, 0.18) if shards else 1.0
    array = jax.random.normal(own_key, dims, jnp.float32) * deviation * loudness
    return jnp.minimum(jnp.maximum(array, -limit), limit).astype(kind)


def setup_inputs(seed: int = 0) -> dict:
    seeds = jax.random.split(jax.random.key(seed), 5)
    coefficients = bell_draw(seeds[0], (NODES, RANK, RHS), 1.0, 6.0, ((0, 32),), jnp.float32)
    transfer = bell_draw(seeds[1], (LEVELS, NODES, RANK, 2 * RANK), (2 * RANK) ** -0.5, 0.375, ((1, 32),), jnp.float32)
    local_bits = place_ends(jax.random.randint(seeds[2], (LOCAL_LEVELS,), 0, NODE_BITS), jax.random.fold_in(seeds[2], 1), 0, NODE_BITS - 1).astype(jnp.int32)
    relabel = jax.random.permutation(seeds[3], ROWS_DEV).astype(jnp.int32)
    return dict(coefficients=coefficients, transfer=transfer, local_bits=local_bits, relabel=relabel)


def combine(node_state, partner_state, transfer_block, lower_side):
    rank_width = node_state.shape[1]
    leading = jnp.where(lower_side, node_state, partner_state)
    trailing = jnp.where(lower_side, partner_state, node_state)
    first_part = jnp.einsum("nrk,nkc->nrc", transfer_block[:, :, :rank_width], leading, precision=lax.Precision.HIGHEST)
    second_part = jnp.einsum("nrk,nkc->nrc", transfer_block[:, :, rank_width:], trailing, precision=lax.Precision.HIGHEST)
    return first_part + second_part


def pair_level(node_state, transfer_block, distance):
    node_index = jnp.arange(node_state.shape[0], dtype=jnp.int32)
    distance = jnp.asarray(distance, dtype=jnp.int32)
    partner = jnp.bitwise_xor(node_index, distance).astype(jnp.int32)
    lower_side = (jnp.bitwise_and(node_index, distance) == 0)[:, None, None]
    partner_state = jnp.take(node_state, partner, axis=0)
    return combine(node_state, partner_state, transfer_block, lower_side)


def local_distance(local_bits, slot_index):
    return jnp.left_shift(jnp.int32(1), local_bits[slot_index]).astype(jnp.int32)


def reference(coefficients, transfer, local_bits, relabel):
    node_state = pair_level(coefficients, transfer[0], local_distance(local_bits, 0))
    node_state = pair_level(node_state, transfer[1], (N_SRC // 2) * N_TGT * NODES_DEV)
    node_state = pair_level(node_state, transfer[2], local_distance(local_bits, 1))
    node_state = pair_level(node_state, transfer[3], N_TGT * NODES_DEV)
    columns = node_state.shape[2]
    blocks = node_state.reshape(N_SRC, N_TGT, ROWS_DEV, columns)
    blocks = jnp.take(blocks, relabel.astype(jnp.int32), axis=2)
    blocks = blocks.reshape(N_SRC, N_TGT, N_TGT, ROWS_DEV // N_TGT, columns)
    blocks = jnp.swapaxes(blocks, 1, 2)
    node_state = blocks.reshape(NODES, RANK, columns)
    node_state = pair_level(node_state, transfer[4], (N_TGT // 2) * NODES_DEV)
    node_state = pair_level(node_state, transfer[5], local_distance(local_bits, 2))
    node_state = pair_level(node_state, transfer[6], NODES_DEV)
    node_state = pair_level(node_state, transfer[7], local_distance(local_bits, 3))
    return node_state
```

```python
import functools

import jax
import jax.numpy as jnp
from jax import lax
from jax.experimental import pallas as pl
from jax.experimental.pallas import tpu as pltpu
from jax.sharding import PartitionSpec as P

F32, BF16 = jnp.float32, jnp.bfloat16
GROUP = 128
CUTS = (1, 1, 1, 1)
WINDOW = 2
VMEM_LIMIT = 40 * 1024 * 1024


def partner_2(shard, axis, mask):
    return lax.ppermute(shard, axis, [(i, i ^ mask) for i in range(lax.axis_size(axis))])


def split2(x):
    high = x.astype(BF16)
    return high, (x - high.astype(F32)).astype(BF16)


def split3(x):
    high = x.astype(BF16)
    rest = x - high.astype(F32)
    middle = rest.astype(BF16)
    return high, middle, (rest - middle.astype(F32)).astype(BF16)


def product(blocks, x):
    half, width = blocks.shape[0] // 2, x.shape[1]
    out = jnp.dot(blocks, jnp.concatenate(split2(x), axis=1), preferred_element_type=F32)
    return (out[:half, :width] + out[:half, width:]) + (out[half:, :width] + out[half:, width:])


def cut_out(ref, node, parts):
    slabs = ref.shape[0]
    width = ref.shape[2] // parts
    lane = node // slabs * width
    return ref[node % slabs, :, lane:lane + width]


def pack_out(ref, state, parts):
    slabs = ref.shape[0]
    for slab in range(slabs):
        row = [state[slab + part * slabs] for part in range(parts)]
        ref[slab] = row[0] if parts == 1 else jnp.concatenate(row, axis=1)


def local_pairs(state, blocks, bit, emit):
    for index in range(state.shape[0] // 2):
        low_bits = jnp.bitwise_and(index, jnp.left_shift(1, bit) - 1)
        low = jnp.left_shift(jnp.right_shift(index, bit), bit + 1) | low_bits
        high = low | jnp.left_shift(1, bit)
        both = jnp.concatenate([state[low], state[high]], axis=0)
        out = product(blocks(low, high), both)
        rank = state.shape[1]
        emit(low, out[:rank])
        emit(high, out[rank:])


def split_blocks(ref):
    rank = ref.shape[2] // 2

    def blocks(low, high):
        return jnp.concatenate(
            [ref[0, low, :rank], ref[0, high, :rank], ref[0, low, rank:], ref[0, high, rank:]], axis=0
        )

    return blocks


def first_kernel(parts, part, bits, x_ref, g_ref, *rest):
    out_ref, before, after = rest[-3:]
    nodes, _, _ = x_ref.shape
    width = x_ref.shape[2] // parts
    for node in range(nodes):
        before[node] = x_ref[node, :, part * width:(part + 1) * width]

    def blocks(low, high):
        top = jnp.concatenate([g_ref[0, low], g_ref[0, high]], axis=0)
        return jnp.concatenate(split2(top), axis=0)

    def emit(node, value):
        after[node] = value

    local_pairs(before, blocks, bits[0], emit)
    pack_out(out_ref, after, parts)


def prepare_kernel(g_ref, _, out_ref):
    rank = g_ref.shape[2]
    for node in range(g_ref.shape[1]):
        high, low = split2(g_ref[0, node])
        out_ref[0, node, :rank] = high
        out_ref[0, node, rank:] = low


def choose_kernel(axis, relabel_ref, _, out_ref):
    rows = out_ref.shape[0]
    count = lax.axis_size(axis)
    half, piece_rows = count // 2, rows // count
    group = lax.axis_index(axis) % half
    for offset in range(half):
        for side in range(2):
            piece = side * half + jnp.bitwise_xor(group, offset)
            start = pl.multiple_of(piece * piece_rows, piece_rows)
            wanted = relabel_ref[pl.ds(start, piece_rows), :]
            column = lax.broadcasted_iota(jnp.int32, (piece_rows, rows), 1)
            place = (offset * 2 + side) * piece_rows
            out_ref[place:place + piece_rows, :] = jnp.where(wanted == column, 1.0, 0.0).astype(BF16)


def cross_node(blocks, own, other, upper):
    leading = jnp.where(upper, other, own)
    trailing = jnp.where(upper, own, other)
    return product(blocks, jnp.concatenate([leading, trailing], axis=0))


def pair_kernel(parts, axis, shift, slot, bits, own, other, g_cross, g_local, out_ref, before, after):
    upper = jnp.bitwise_and(jnp.right_shift(lax.axis_index(axis), shift), 1) == 1
    for node in range(before.shape[0]):
        before[node] = cross_node(
            g_cross[0, node], cut_out(own, node, parts), cut_out(other, node, parts), upper
        )

    def emit(node, value):
        after[node] = value

    local_pairs(before, split_blocks(g_local), bits[slot], emit)
    pack_out(out_ref, after, parts)


def last_kernel(parts, part, axis, shift, slot, bits, own, other, g_cross, g_local, *rest):
    out_ref, before, after = rest[-3:]
    earlier = rest[0]
    upper = jnp.bitwise_and(jnp.right_shift(lax.axis_index(axis), shift), 1) == 1
    for node in range(before.shape[0]):
        before[node] = cross_node(
            g_cross[0, node], cut_out(own, node, parts), cut_out(other, node, parts), upper
        )

    def emit(node, value):
        after[node] = value

    local_pairs(before, split_blocks(g_local), bits[slot], emit)
    width = out_ref.shape[2] // parts
    for node in range(before.shape[0]):
        if part:
            out_ref[node] = earlier[node]
        out_ref[node, :, part * width:(part + 1) * width] = after[node]


def relabel_kernel(parts, axis, shift, own, other, g_cross, chosen, *rest):
    outs, spread = rest[:-1], rest[-1]
    upper = jnp.bitwise_and(jnp.right_shift(lax.axis_index(axis), shift), 1) == 1
    rank = g_cross.shape[2] // 2
    nodes, width = g_cross.shape[1], spread.shape[1] // 3
    for node in range(nodes):
        value = cross_node(
            g_cross[0, node], cut_out(own, node, parts), cut_out(other, node, parts), upper
        )
        spread[node * rank:(node + 1) * rank] = jnp.concatenate(split3(value), axis=1)
    piece_rows = nodes * rank // (2 * len(outs))
    for index, out_ref in enumerate(outs):
        for side in range(2):
            place = (index * 2 + side) * piece_rows
            out = jnp.dot(chosen[place:place + piece_rows], spread[...], preferred_element_type=F32)
            out = (out[:, :width] + out[:, width:2 * width]) + out[:, 2 * width:]
            rows = piece_rows // parts
            row = [out[part * rows:(part + 1) * rows] for part in range(parts)]
            out_ref[side] = row[0] if parts == 1 else jnp.concatenate(row, axis=1)


def gather_kernel(parts, axis, slot, bits, g_cross, g_local, *rest):
    received, (out_ref, both, before, after) = rest[:-4], rest[-4:]
    me = lax.axis_index(axis)
    rows = both.shape[1]
    piece_rows = rows // len(received)
    packed = piece_rows // parts
    width = both.shape[2]
    for offset, ref in enumerate(received):
        start = pl.multiple_of(jnp.bitwise_xor(me, offset) * piece_rows, piece_rows)
        for side in range(2):
            for part in range(parts):
                both[side, pl.ds(start + part * packed, packed), :] = ref[
                    side, :, part * width:(part + 1) * width
                ]
    rank = before.shape[1]
    for node in range(before.shape[0]):
        span = slice(node * rank, (node + 1) * rank)
        before[node] = product(
            g_cross[0, node], jnp.concatenate([both[0, span], both[1, span]], axis=0)
        )

    def emit(node, value):
        after[node] = value

    local_pairs(before, split_blocks(g_local), bits[slot], emit)
    pack_out(out_ref, after, parts)


SMEM = pl.BlockSpec(memory_space=pltpu.SMEM)
ANY = pl.BlockSpec(memory_space=pl.ANY)


def whole(shape):
    return pl.BlockSpec(shape, lambda i: (0,) * len(shape))


def level_of(array, level):
    return pl.BlockSpec((1,) + array.shape[1:], lambda i: (level, 0, 0, 0))


def call(kernel, out_shape, in_specs, out_specs, scratch, flops, **more):
    return pl.pallas_call(
        kernel,
        out_shape=out_shape,
        grid=(1,),
        in_specs=in_specs,
        out_specs=out_specs,
        scratch_shapes=scratch,
        compiler_params=pltpu.CompilerParams(vmem_limit_bytes=VMEM_LIMIT),
        cost_estimate=pl.CostEstimate(flops=flops, bytes_accessed=4 * 1024 * 1024, transcendentals=0),
        **more,
    )


def on_device(coefficients, transfer, local_bits, relabel):
    nodes, rank, columns = coefficients.shape
    rows = nodes * rank
    n_src, n_tgt = lax.axis_size("src"), lax.axis_size("tgt")
    src_far, tgt_far = n_src // 2, n_tgt // 2
    shape = jax.ShapeDtypeStruct

    chunks = [(group, part, parts) for group, parts in enumerate(CUTS) for part in range(parts)]
    state, far = [], []
    blocks = chosen = None

    def packed_shape(parts):
        return (nodes // parts, rank, GROUP)

    def scratch(parts):
        return [pltpu.VMEM((nodes, rank, GROUP // parts), F32)] * 2

    def flops(levels, parts):
        return levels * 8 * rows * 2 * rank * GROUP // parts

    for index, (group, part, parts) in enumerate(chunks):
        held = [far[index - WINDOW]] if index >= WINDOW else []
        out = call(
            functools.partial(first_kernel, parts, part),
            shape(packed_shape(parts), F32),
            [
                SMEM,
                pl.BlockSpec((nodes, rank, GROUP), lambda i, group=group: (0, 0, group)),
                level_of(transfer, 0),
            ] + [ANY] * len(held),
            whole(packed_shape(parts)),
            scratch(parts),
            flops(1, parts),
        )(local_bits, coefficients, transfer, *held)
        state.append(out)
        far.append(partner_2(out, "src", src_far))
        if index == 0:
            levels = transfer.shape[0]
            blocks = pl.pallas_call(
                prepare_kernel,
                out_shape=shape((levels, nodes, 2 * rank, 2 * rank), BF16),
                grid=(levels - 1,),
                in_specs=[pl.BlockSpec((1,) + transfer.shape[1:], lambda i: (i + 1, 0, 0, 0)), ANY],
                out_specs=pl.BlockSpec((1, nodes, 2 * rank, 2 * rank), lambda i: (i + 1, 0, 0, 0)),
                compiler_params=pltpu.CompilerParams(vmem_limit_bytes=VMEM_LIMIT),
                cost_estimate=pl.CostEstimate(flops=0, bytes_accessed=16 * 1024 * 1024, transcendentals=0),
            )(transfer, out)
            chosen = call(
                functools.partial(choose_kernel, "tgt"),
                shape((rows, rows), BF16),
                [whole((rows, 1)), ANY],
                whole((rows, rows)),
                [],
                0,
            )(relabel.reshape(rows, 1), out)

    result = partial = None
    for index, (group, part, parts) in enumerate(chunks):
        packed = packed_shape(parts)
        own = call(
            functools.partial(pair_kernel, parts, "src", src_far.bit_length() - 1, 1),
            shape(packed, F32),
            [SMEM, whole(packed), whole(packed), level_of(blocks, 1), level_of(blocks, 2)],
            whole(packed),
            scratch(parts),
            flops(2, parts),
        )(local_bits, state[index], far[index], blocks, blocks)
        near = partner_2(own, "src", 1)
        piece = (2, rows // n_tgt // parts, GROUP)
        pieces = call(
            functools.partial(relabel_kernel, parts, "src", 0),
            [shape(piece, F32)] * tgt_far,
            [whole(packed), whole(packed), level_of(blocks, 3), whole((rows, rows))],
            [whole(piece)] * tgt_far,
            [pltpu.VMEM((rows, 3 * GROUP // parts), BF16)],
            flops(1, parts) + 6 * rows * rows * GROUP // parts,
        )(own, near, blocks, chosen)
        received = [
            pieces[0] if offset == 0 else partner_2(pieces[offset % tgt_far], "tgt", offset)
            for offset in range(n_tgt)
        ]
        own = call(
            functools.partial(gather_kernel, parts, "tgt", 2),
            shape(packed, F32),
            [SMEM, level_of(blocks, 4), level_of(blocks, 5)] + [whole(piece)] * n_tgt,
            whole(packed),
            [pltpu.VMEM((2, rows, GROUP // parts), F32)] + scratch(parts),
            flops(2, parts),
        )(local_bits, blocks, blocks, *received)
        near = partner_2(own, "tgt", 1)
        args = [local_bits, own, near, blocks, blocks]
        specs = [SMEM, whole(packed), whole(packed), level_of(blocks, 6), level_of(blocks, 7)]
        aliases = {}
        if part:
            args.append(partial)
            specs.append(whole((nodes, rank, GROUP)))
        final = part == parts - 1
        if final and group:
            aliases = {len(args): 0}
            args.append(result)
            specs.append(ANY)
        out = call(
            functools.partial(last_kernel, parts, part, "tgt", 0, 3),
            shape((nodes, rank, columns if final else GROUP), F32),
            specs,
            pl.BlockSpec((nodes, rank, GROUP), lambda i, at=group if final else 0: (0, 0, at)),
            scratch(parts),
            flops(2, parts),
            input_output_aliases=aliases,
        )(*args)
        if final:
            result = out
        else:
            partial = out
    return result


def solution(mesh):
    placed = (P(("src", "tgt"), None, None), P(None, ("src", "tgt"), None, None), P(), P())
    return jax.shard_map(
        on_device,
        mesh=mesh,
        in_specs=placed,
        out_specs=P(("src", "tgt"), None, None),
        check_vma=False,
    )
```

```python
import functools

import jax
import jax.numpy as jnp
from jax import lax
from jax.experimental import pallas as pl
from jax.experimental.pallas import tpu as pltpu
from jax.sharding import PartitionSpec as P

F32, BF16 = jnp.float32, jnp.bfloat16
GROUP = 128
CUTS = (1, 1, 1, 1)
PAD = 8
PAD_X = 8
WINDOW = 2
CORE_SPLIT = 2
Y_CUTS = (2, 2, 2, 2)
JOINT = 0
STAGES = (1, 3, 4, 6)
VMEM_LIMIT = 16 * 1024 * 1024
FIRST_LIMIT = 62 * 1024 * 1024


def partner_2(shard, axis, mask):
    return lax.ppermute(shard, axis, [(i, i ^ mask) for i in range(lax.axis_size(axis))])


def split2(x):
    high = x.astype(BF16)
    return high, (x - high.astype(F32)).astype(BF16)


def split3(x):
    high = x.astype(BF16)
    rest = x - high.astype(F32)
    middle = rest.astype(BF16)
    return high, middle, (rest - middle.astype(F32)).astype(BF16)


def product(blocks, x):
    half, width = blocks.shape[0] // 2, x.shape[1]
    out = jnp.dot(blocks, jnp.concatenate(split2(x), axis=1), preferred_element_type=F32)
    return (out[:half, :width] + out[:half, width:]) + (out[half:, :width] + out[half:, width:])


def unpack(refs, first, count, parts, extra=0):
    each = refs[0].shape[0] - extra
    width = refs[0].shape[1] // parts
    run = each * len(refs)
    lane = first // run * width
    place = first % run
    return refs[place // each][place % each:place % each + count, lane:lane + width]


def pack(out_ref, rows, parts):
    run = out_ref.shape[0]
    out_ref[...] = jnp.concatenate([rows[part * run:(part + 1) * run, :] for part in range(parts)], axis=1)


def local_level(state, rank, blocks, bit, put, lanes=slice(None)):
    nodes = state.shape[0] // rank
    for index in range(nodes // 2):
        low_bits = jnp.bitwise_and(index, jnp.left_shift(1, bit) - 1)
        low = jnp.left_shift(jnp.right_shift(index, bit), bit + 1) | low_bits
        high = low | jnp.left_shift(1, bit)
        spans = [pl.ds(pl.multiple_of(node * rank, rank), rank) for node in (low, high)]
        both = jnp.concatenate([state[span, lanes] for span in spans], axis=0)
        out = product(blocks(low, high), both)
        put(spans[0], out[:rank])
        put(spans[1], out[rank:])


def split_blocks(ref, level):
    rank = ref.shape[2] // 2

    def blocks(low, high):
        return jnp.concatenate(
            [ref[level, low, :rank], ref[level, high, :rank], ref[level, low, rank:], ref[level, high, rank:]],
            axis=0,
        )

    return blocks


def packed_level(state, blocks, level, bit, outs, after, parts):
    rank = blocks.shape[2] // 2
    target = outs[0] if parts == 1 and len(outs) == 1 else after

    def put(span, value):
        target[span, :] = value

    local_level(state, rank, split_blocks(blocks, level), bit, put)
    if target is after:
        each = outs[0].shape[0]
        run = each * len(outs)
        for index, out_ref in enumerate(outs):
            row = [after[part * run + index * each:part * run + (index + 1) * each] for part in range(parts)]
            out_ref[...] = row[0] if parts == 1 else jnp.concatenate(row, axis=1)


def first_kernel(chunks, bits, x_hbm, g_hbm, *rest):
    outs, (x_ref, g_ref, after, arrived) = rest[-4 - len(chunks):-4], rest[-4:]
    nodes, rank, _ = x_ref.shape
    lanes = outs[0].shape[1]
    first, groups = chunks[0][0], x_ref.shape[2] // lanes
    x_copy = pltpu.make_async_copy(
        x_hbm.at[:, :, first * lanes:(first + groups) * lanes], x_ref, arrived.at[0]
    )
    g_copy = pltpu.make_async_copy(g_hbm.at[0], g_ref, arrived.at[1])
    x_copy.start()
    g_copy.start()
    x_copy.wait()
    g_copy.wait()
    state = x_ref.reshape(nodes * rank, x_ref.shape[2])

    def blocks(low, high):
        top = jnp.concatenate([g_ref[low], g_ref[high]], axis=0)
        return jnp.concatenate(split2(top), axis=0)

    for (group, part, parts), out_ref in zip(chunks, outs):
        width = lanes // parts
        begin = (group - first) * lanes + part * width
        run = out_ref.shape[0] - PAD

        def put(span, value):
            if parts == 1:
                out_ref[span, :] = value
            else:
                after[span, :width] = value

        local_level(state, rank, blocks, bits[0], put, slice(begin, begin + width))
        if parts > 1:
            out_ref[:run, :] = jnp.concatenate(
                [after[at * run:(at + 1) * run, :width] for at in range(parts)], axis=1
            )
        out_ref[run:, :] = jnp.zeros((PAD, lanes), F32)


def release_kernel(*_):
    pass


def prepare_kernel(g_hbm, *rest):
    outs, (g_ref, arrived) = rest[-2 - len(STAGES):-2], rest[-2:]
    levels, nodes, rank, _ = g_ref.shape
    copies = [
        pltpu.make_async_copy(g_hbm.at[level + 1], g_ref.at[level], arrived.at[level])
        for level in range(levels)
    ]
    for copy in copies:
        copy.start()
    for first, out_ref in zip(STAGES, outs):
        for offset in range(out_ref.shape[0]):
            level = first - 1 + offset
            copies[level].wait()

            def split(node, carry):
                high, low = split2(g_ref[level, node])
                out_ref[offset, node, :rank] = high
                out_ref[offset, node, rank:] = low
                return carry

            lax.fori_loop(0, nodes, split, 0)


def choose_kernel(axis, relabel_ref, *rest):
    out_ref = rest[-1]
    rows = out_ref.shape[0]
    count = lax.axis_size(axis)
    half, piece_rows = count // 2, rows // count
    group = lax.axis_index(axis) % half
    for offset in range(half):
        for side in range(2):
            piece = side * half + jnp.bitwise_xor(group, offset)
            start = pl.multiple_of(piece * piece_rows, piece_rows)
            wanted = relabel_ref[pl.ds(start, piece_rows), :]
            column = lax.broadcasted_iota(jnp.int32, (piece_rows, rows), 1)
            place = (offset * 2 + side) * piece_rows
            out_ref[place:place + piece_rows, :] = jnp.where(wanted == column, 1.0, 0.0).astype(BF16)


def cross_level(put, axis, shift, blocks, level, take_own, take_other):
    upper = jnp.bitwise_and(jnp.right_shift(lax.axis_index(axis), shift), 1) == 1
    nodes, rank = blocks.shape[1], blocks.shape[2] // 2
    for node in range(nodes):
        own, other = take_own(node * rank, rank), take_other(node * rank, rank)
        leading = jnp.where(upper, other, own)
        trailing = jnp.where(upper, own, other)
        value = product(blocks[level, node], jnp.concatenate([leading, trailing], axis=0))
        put(node * rank, rank, value)


def put_rows(ref):
    def put(first, count, value):
        ref[first:first + count, :] = value

    return put


def pair_kernel(parts, cuts, axis, shift, level, slot, bits, blocks, own, other, *rest):
    outs, before, after = rest[-2 - cuts:-2], *rest[-2:]
    cross_level(
        put_rows(before), axis, shift, blocks, level,
        lambda first, count: unpack([own], first, count, parts, PAD),
        lambda first, count: unpack([other], first, count, parts, PAD),
    )
    packed_level(before, blocks, level + 1, bits[slot], outs, after, parts)


def last_kernel(parts, part, done, axis, shift, level, slot, bits, blocks, *rest):
    own, other, rest = rest[:CORE_SPLIT], rest[CORE_SPLIT:2 * CORE_SPLIT], rest[2 * CORE_SPLIT:]
    out_ref, before, after, sent = rest[-4:]
    nodes, rank = blocks.shape[1], blocks.shape[2] // 2
    width = before.shape[1]
    lanes = after.shape[1]
    earlier = rest[:1] if part else ()
    copies = [
        pltpu.make_async_copy(
            ref.reshape(nodes, rank, lanes), out_ref.at[:, :, at * lanes:(at + 1) * lanes], sent.at[at]
        )
        for at, ref in enumerate([*rest[len(earlier):len(earlier) + done], after] if done else [])
    ]
    for copy in copies[:-1]:
        copy.start()
    cross_level(
        put_rows(before), axis, shift, blocks, level,
        lambda first, count: unpack(own, first, count, parts),
        lambda first, count: unpack(other, first, count, parts),
    )
    target = after if done else out_ref
    for ref in earlier:
        target[...] = ref[...]

    def put(span, value):
        target[span, part * width:(part + 1) * width] = value

    local_level(before, rank, split_blocks(blocks, level + 1), bits[slot], put)
    for copy in copies[-1:]:
        copy.start()
    for copy in copies:
        copy.wait()


def relabel_kernel(parts, cuts, count, joint, axis, shift, level, blocks, chosen, *rest):
    own, other = rest[:cuts], rest[cuts:2 * cuts]
    spread = rest[-1]
    outs = [[rest[-3].at[offset]] for offset in range(count)] if joint else [[ref] for ref in rest[-1 - count:-1]]
    if joint:
        outs[1 % count].append(rest[-2])
    width = spread.shape[1] // 3

    def put(first, size, value):
        spread[first:first + size] = jnp.concatenate(split3(value), axis=1)

    cross_level(
        put, axis, shift, blocks, level,
        lambda first, size: unpack(own, first, size, parts),
        lambda first, size: unpack(other, first, size, parts),
    )
    piece_rows = spread.shape[0] // (2 * count)
    for index, targets in enumerate(outs):
        for side in range(2):
            place = (index * 2 + side) * piece_rows
            out = jnp.dot(chosen[place:place + piece_rows], spread[...], preferred_element_type=F32)
            out = (out[:, :width] + out[:, width:2 * width]) + out[:, 2 * width:]
            for target in targets:
                pack(target.at[side, :piece_rows // parts], out, parts)


def gather_kernel(parts, count, picks, axis, level, slot, bits, blocks, *rest):
    received, outs = rest[:count], rest[-3 - CORE_SPLIT:-3]
    both, before, after = rest[-3:]
    me = lax.axis_index(axis)
    rows, width = both.shape[1:]
    piece_rows = rows // count
    run = piece_rows // parts
    for offset, ref in enumerate(received):
        ref = ref if picks[offset] is None else ref.at[picks[offset]]
        start = pl.multiple_of(jnp.bitwise_xor(me, offset) * piece_rows, piece_rows)
        for side in range(2):
            for part in range(parts):
                both[side, pl.ds(start + part * run, run), :] = ref[
                    side, :run, part * width:(part + 1) * width
                ]
    nodes, rank = blocks.shape[1], blocks.shape[2] // 2
    for node in range(nodes):
        span = slice(node * rank, (node + 1) * rank)
        before[span] = product(
            blocks[level, node], jnp.concatenate([both[0, span], both[1, span]], axis=0)
        )
    packed_level(before, blocks, level + 1, bits[slot], outs, after, parts)


SMEM = pl.BlockSpec(memory_space=pltpu.SMEM)
VMEM = pl.BlockSpec(memory_space=pltpu.VMEM)
HBM = pl.BlockSpec(memory_space=pltpu.HBM)
ANY = pl.BlockSpec(memory_space=pl.ANY)


def on_device(coefficients, transfer, local_bits, relabel):
    levels = transfer.shape[0]
    nodes, rank, columns = coefficients.shape
    rows = nodes * rank
    n_src, n_tgt = lax.axis_size("src"), lax.axis_size("tgt")
    src_far, tgt_far = n_src // 2, n_tgt // 2
    shape = jax.ShapeDtypeStruct
    chunks = [(group, part, parts) for group, parts in enumerate(CUTS) for part in range(parts)]
    store = {}

    def run(kernel, out_shape, in_specs, out_specs, scratch, args, aliases=None, limit=VMEM_LIMIT):
        extra = [store["token"]] if "token" in store else []
        out = pl.pallas_call(
            kernel,
            out_shape=out_shape,
            in_specs=list(in_specs) + [ANY] * len(extra),
            out_specs=out_specs,
            scratch_shapes=scratch,
            input_output_aliases=aliases or {},
            compiler_params=pltpu.CompilerParams(vmem_limit_bytes=limit),
            cost_estimate=pl.CostEstimate(flops=0, bytes_accessed=0, transcendentals=0),
        )(*args, *extra)
        store["token"] = out[0]
        return out

    def packed(parts, count=1):
        return [shape((rows // parts // count, GROUP), F32)] * count

    def narrow(parts, count):
        return [pltpu.VMEM((rows, GROUP // parts), F32)] * count

    def step_a(index):
        wanted = chunks[1:] if index else chunks[:1]
        groups = wanted[-1][0] - wanted[0][0] + 1
        out = run(
            functools.partial(first_kernel, tuple(wanted)),
            [shape((rows // parts + PAD, GROUP), F32) for _, _, parts in wanted],
            [SMEM, HBM, HBM],
            [VMEM] * len(wanted),
            [
                pltpu.VMEM((nodes, rank, groups * GROUP), F32),
                pltpu.VMEM(transfer.shape[1:], F32),
                pltpu.VMEM((rows, GROUP), F32),
                pltpu.SemaphoreType.DMA((2,)),
            ],
            [local_bits, coefficients, transfer],
            limit=FIRST_LIMIT,
        )
        for offset, array in enumerate(out):
            store["whole", index + offset] = array
        if index < WINDOW:
            store["far", index] = partner_2(out[0], "src", src_far)

    def step_p(_):
        ends = STAGES[1:] + (levels,)
        blocks = run(
            prepare_kernel,
            [shape((end - first, nodes, 2 * rank, 2 * rank), BF16) for first, end in zip(STAGES, ends)],
            [HBM],
            [VMEM] * len(STAGES),
            [pltpu.VMEM((levels - 1,) + transfer.shape[1:], F32), pltpu.SemaphoreType.DMA((levels - 1,))],
            [transfer],
        )
        for first, array in zip(STAGES, blocks):
            store["blocks", first] = array

    def step_q(_):
        store["chosen"] = run(
            functools.partial(choose_kernel, "tgt"),
            [shape((rows, rows), BF16)],
            [VMEM],
            [VMEM],
            [],
            [relabel.reshape(rows, 1)],
        )[0]

    def step_r(index):
        array = store["whole", index]
        array = run(
            release_kernel,
            [shape(array.shape, F32)],
            [ANY, ANY],
            [ANY],
            [],
            [array, store["far", index - WINDOW]],
            aliases={0: 0},
        )[0]
        store["whole", index] = array
        store["far", index] = partner_2(array, "src", src_far)

    def step_b(index):
        _, _, parts = chunks[index]
        cuts = Y_CUTS[index]
        ended = []
        own = run(
            functools.partial(pair_kernel, parts, cuts, "src", src_far.bit_length() - 1, 0, 1),
            packed(parts, cuts),
            [SMEM, VMEM, VMEM, VMEM] + [ANY] * len(ended),
            [VMEM] * cuts,
            narrow(parts, 2),
            [local_bits, store["blocks", 1], store["whole", index], store["far", index], *ended],
        )
        store["own", index] = own
        store["near", index] = [partner_2(piece, "src", 1) for piece in own]

    def step_c(index):
        _, _, parts = chunks[index]
        cuts = Y_CUTS[index]
        joint = index < JOINT
        piece = (2, rows // n_tgt // parts, GROUP)
        pieces = run(
            functools.partial(relabel_kernel, parts, cuts, tgt_far, joint, "src", 0, 0),
            [shape((tgt_far, 2, piece[1] + PAD_X, GROUP), F32), shape(piece, F32)] if joint else [shape(piece, F32)] * tgt_far,
            [VMEM] * (2 + 2 * cuts),
            [VMEM] * (2 if joint else tgt_far),
            [pltpu.VMEM((rows, 3 * GROUP // parts), BF16)],
            [store["blocks", 3], store["chosen"], *store["own", index], *store["near", index]],
        )
        for offset, piece in enumerate(pieces):
            store["piece", index, offset] = piece

    def step_t(index):
        store["moved", index, 1] = partner_2(store["piece", index, 1 % tgt_far], "tgt", 1)

    def step_x(index):
        if index >= JOINT:
            for offset in range(2, n_tgt):
                store["moved", index, offset] = partner_2(
                    store["piece", index, offset % tgt_far], "tgt", offset
                )
            return
        joint = store["piece", index, 0]
        for offset in range(2, n_tgt, 2):
            first = offset % tgt_far
            both = joint if tgt_far == 2 else joint[first:first + 2]
            store["moved", index, offset] = partner_2(both, "tgt", offset)

    def step_s(index):
        if index < JOINT:
            for offset in range(2, n_tgt, 2):
                store["moved", index, offset + 1] = partner_2(store["moved", index, offset][1], "tgt", 1)

    def step_d(index):
        _, _, parts = chunks[index]
        joint = index < JOINT
        picks = tuple(0 if joint and offset % 2 == 0 else None for offset in range(n_tgt))
        store["mid", index] = run(
            functools.partial(gather_kernel, parts, n_tgt, picks, "tgt", 0, 2),
            packed(parts, CORE_SPLIT),
            [SMEM, VMEM] + [VMEM] * n_tgt,
            [VMEM] * CORE_SPLIT,
            [pltpu.VMEM((2, rows, GROUP // parts), F32)] + narrow(parts, 2),
            [
                local_bits, store["blocks", 4], store["piece", index, 0],
                *(store["moved", index, offset] for offset in range(1, n_tgt)),
            ],
        )
        store["core", index] = [partner_2(piece, "tgt", 1) for piece in store["mid", index]]

    def step_e(index):
        group, part, parts = chunks[index]
        final = index == len(chunks) - 1
        earlier = [store["out", index - 1]] if part else []
        if final:
            earlier += [store["out", chunks.index((at, count - 1, count))] for at, count in enumerate(CUTS[:-1])]
        store["out", index] = run(
            functools.partial(last_kernel, parts, part, len(CUTS) - 1 if final else 0, "tgt", 0, 0, 3),
            [shape((nodes, rank, columns) if final else (rows, GROUP), F32)],
            [SMEM, VMEM] + [VMEM] * (2 * CORE_SPLIT + len(earlier)),
            [HBM if final else VMEM],
            narrow(parts, 1) + [pltpu.VMEM((rows, GROUP), F32), pltpu.SemaphoreType.DMA((len(CUTS),))],
            [local_bits, store["blocks", 6], *store["mid", index], *store["core", index], *earlier],
        )[0]

    steps = {
        "A": step_a, "P": step_p, "Q": step_q, "R": step_r,
        "B": step_b, "C": step_c, "T": step_t, "X": step_x, "S": step_s, "D": step_d, "E": step_e,
    }

    def follow(names):
        for name in names:
            steps[name[0]](int(name[1:]))

    kept = ("piece", "moved", "out")

    def apart(names):
        def work():
            before = dict(store)
            follow(names)
            made = {key: value for key, value in store.items() if before.get(key) is not value and key[0] in kept}
            keys.extend(key for key in made if key not in keys)
            store.clear()
            store.update(before)
            return list(made.values())

        keys = []
        shapes = jax.eval_shape(work)
        made = lax.cond(
            local_bits[0] >= 0, work, lambda: jax.tree.map(lambda x: jnp.zeros(x.shape, x.dtype), shapes)
        )
        store.update(zip(keys, made))
        store["token"] = made[0]

    for names in ORDER:
        if isinstance(names, str):
            follow([names])
        else:
            apart(names)
    return store["out", len(chunks) - 1]


ORDER = (
    'A0',
    'A1',
    'P0',
    'Q0',
    'R2',
    'B0',
    'R3',
    'B1',
    'C0',
    'T0',
    'X0',
    'B2',
    'C1',
    'T1',
    'X1',
    'D0',
    'B3',
    'C2',
    'T2',
    'X2',
    'D1',
    'E0',
    'C3',
    'T3',
    'X3',
    'D2',
    'E1',
    'D3',
    'E2',
    'E3',
)


def solution(mesh):
    placed = (P(("src", "tgt"), None, None), P(None, ("src", "tgt"), None, None), P(), P())
    return jax.shard_map(
        on_device,
        mesh=mesh,
        in_specs=placed,
        out_specs=P(("src", "tgt"), None, None),
        check_vma=False,
    )
```

```python
import functools

import jax
import jax.numpy as jnp
from jax import lax
from jax.experimental import pallas as pl
from jax.experimental.pallas import tpu as pltpu
from jax.sharding import PartitionSpec as P

F32, BF16 = jnp.float32, jnp.bfloat16
GROUP = 128
CUTS = (1, 1, 1, 1)
PAD = 8
PAD_X = 0
LAG = (0, 2, 2, 2)
CORE_SPLIT = 1
Y_CUTS = (2, 2, 2, 1)
JOINT = 3
STAGES = (1, 3, 4, 6)
VMEM_LIMIT = 16 * 1024 * 1024
FIRST_LIMIT = 62 * 1024 * 1024


def partner_2(shard, axis, mask):
    return lax.ppermute(shard, axis, [(i, i ^ mask) for i in range(lax.axis_size(axis))])


def split2(x):
    high = x.astype(BF16)
    return high, (x - high.astype(F32)).astype(BF16)


def product(blocks, x):
    half, width = blocks.shape[0] // 2, x.shape[1]
    out = jnp.dot(blocks, jnp.concatenate(split2(x), axis=1), preferred_element_type=F32)
    return (out[:half, :width] + out[:half, width:]) + (out[half:, :width] + out[half:, width:])


def unpack(refs, first, count, parts, extra=0):
    each = refs[0].shape[0] - extra
    width = refs[0].shape[1] // parts
    run = each * len(refs)
    lane = first // run * width
    place = first % run
    return refs[place // each][place % each:place % each + count, lane:lane + width]


def pack(out_ref, rows, parts):
    run = out_ref.shape[0]
    out_ref[...] = jnp.concatenate([rows[part * run:(part + 1) * run, :] for part in range(parts)], axis=1)


def local_level(state, rank, blocks, bit, put, lanes=slice(None)):
    nodes = state.shape[0] // rank
    for index in range(nodes // 2):
        low_bits = jnp.bitwise_and(index, jnp.left_shift(1, bit) - 1)
        low = jnp.left_shift(jnp.right_shift(index, bit), bit + 1) | low_bits
        high = low | jnp.left_shift(1, bit)
        spans = [pl.ds(pl.multiple_of(node * rank, rank), rank) for node in (low, high)]
        both = jnp.concatenate([state[span, lanes] for span in spans], axis=0)
        out = product(blocks(low, high), both)
        put(spans[0], out[:rank])
        put(spans[1], out[rank:])


def split_blocks(ref, level):
    rank = ref.shape[2] // 2

    def blocks(low, high):
        return jnp.concatenate(
            [ref[level, low, :rank], ref[level, high, :rank], ref[level, low, rank:], ref[level, high, rank:]],
            axis=0,
        )

    return blocks


def packed_level(state, blocks, level, bit, outs, after, parts):
    rank = blocks.shape[2] // 2
    target = outs[0] if parts == 1 and len(outs) == 1 else after

    def put(span, value):
        target[span, :] = value

    local_level(state, rank, split_blocks(blocks, level), bit, put)
    if target is after:
        each = outs[0].shape[0]
        run = each * len(outs)
        for index, out_ref in enumerate(outs):
            row = [after[part * run + index * each:part * run + (index + 1) * each] for part in range(parts)]
            out_ref[...] = row[0] if parts == 1 else jnp.concatenate(row, axis=1)


def first_kernel(chunks, bits, x_hbm, g_hbm, *rest):
    outs, (x_ref, g_ref, after, arrived) = rest[-4 - len(chunks):-4], rest[-4:]
    nodes, rank, _ = x_ref.shape
    lanes = outs[0].shape[1]
    first, groups = chunks[0][0], x_ref.shape[2] // lanes
    x_copy = pltpu.make_async_copy(
        x_hbm.at[:, :, first * lanes:(first + groups) * lanes], x_ref, arrived.at[0]
    )
    g_copy = pltpu.make_async_copy(g_hbm.at[0], g_ref, arrived.at[1])
    x_copy.start()
    g_copy.start()
    x_copy.wait()
    g_copy.wait()
    state = x_ref.reshape(nodes * rank, x_ref.shape[2])

    def blocks(low, high):
        top = jnp.concatenate([g_ref[low], g_ref[high]], axis=0)
        return jnp.concatenate(split2(top), axis=0)

    for (group, part, parts), out_ref in zip(chunks, outs):
        width = lanes // parts
        begin = (group - first) * lanes + part * width
        run = out_ref.shape[0] - PAD

        def put(span, value):
            if parts == 1:
                out_ref[span, :] = value
            else:
                after[span, :width] = value

        local_level(state, rank, blocks, bits[0], put, slice(begin, begin + width))
        if parts > 1:
            out_ref[:run, :] = jnp.concatenate(
                [after[at * run:(at + 1) * run, :width] for at in range(parts)], axis=1
            )
        out_ref[run:, :] = jnp.zeros((PAD, lanes), F32)


def release_kernel(*_):
    pass


def cross_kernel(joint, *rest):
    rest[-1][...] = joint[1]


def prepare_kernel(g_hbm, *rest):
    outs, (g_ref, arrived) = rest[-2 - len(STAGES):-2], rest[-2:]
    levels, nodes, rank, _ = g_ref.shape
    copies = [
        pltpu.make_async_copy(g_hbm.at[level + 1], g_ref.at[level], arrived.at[level])
        for level in range(levels)
    ]
    for copy in copies:
        copy.start()
    for first, out_ref in zip(STAGES, outs):
        for offset in range(out_ref.shape[0]):
            level = first - 1 + offset
            copies[level].wait()

            def split(node, carry):
                high, low = split2(g_ref[level, node])
                out_ref[offset, node, :rank] = high
                out_ref[offset, node, rank:] = low
                return carry

            lax.fori_loop(0, nodes, split, 0)


def choose_kernel(axis, relabel_ref, *rest):
    out_ref = rest[-1]
    rows = out_ref.shape[0]
    count = lax.axis_size(axis)
    half, piece_rows = count // 2, rows // count
    group = lax.axis_index(axis) % half
    for offset in range(half):
        for side in range(2):
            piece = side * half + jnp.bitwise_xor(group, offset)
            start = pl.multiple_of(piece * piece_rows, piece_rows)
            wanted = relabel_ref[pl.ds(start, piece_rows), :]
            column = lax.broadcasted_iota(jnp.int32, (piece_rows, rows), 1)
            place = (offset * 2 + side) * piece_rows
            out_ref[place:place + piece_rows, :] = jnp.where(wanted == column, 1.0, 0.0).astype(BF16)


def cross_level(put, axis, shift, blocks, level, take_own, take_other):
    upper = jnp.bitwise_and(jnp.right_shift(lax.axis_index(axis), shift), 1) == 1
    nodes, rank = blocks.shape[1], blocks.shape[2] // 2
    for node in range(nodes):
        own, other = take_own(node * rank, rank), take_other(node * rank, rank)
        leading = jnp.where(upper, other, own)
        trailing = jnp.where(upper, own, other)
        value = product(blocks[level, node], jnp.concatenate([leading, trailing], axis=0))
        put(node * rank, rank, value)


def put_rows(ref):
    def put(first, count, value):
        ref[first:first + count, :] = value

    return put


def pair_kernel(parts, cuts, axis, shift, level, slot, bits, blocks, own, other, *rest):
    outs, before, after = rest[-2 - cuts:-2], *rest[-2:]
    cross_level(
        put_rows(before), axis, shift, blocks, level,
        lambda first, count: unpack([own], first, count, parts, PAD),
        lambda first, count: unpack([other], first, count, parts, PAD),
    )
    packed_level(before, blocks, level + 1, bits[slot], outs, after, parts)


def last_kernel(parts, part, done, axis, shift, level, slot, bits, blocks, *rest):
    own, other, rest = rest[:CORE_SPLIT], rest[CORE_SPLIT:2 * CORE_SPLIT], rest[2 * CORE_SPLIT:]
    out_ref, before, after, sent = rest[-4:]
    nodes, rank = blocks.shape[1], blocks.shape[2] // 2
    width = before.shape[1]
    lanes = after.shape[1]
    earlier = rest[:1] if part else ()
    copies = [
        pltpu.make_async_copy(
            ref.reshape(nodes, rank, lanes), out_ref.at[:, :, at * lanes:(at + 1) * lanes], sent.at[at]
        )
        for at, ref in enumerate([*rest[len(earlier):len(earlier) + done], after] if done else [])
    ]
    for copy in copies[:-1]:
        copy.start()
    cross_level(
        put_rows(before), axis, shift, blocks, level,
        lambda first, count: unpack(own, first, count, parts),
        lambda first, count: unpack(other, first, count, parts),
    )
    target = after if done else out_ref
    for ref in earlier:
        target[...] = ref[...]

    def put(span, value):
        target[span, part * width:(part + 1) * width] = value

    local_level(before, rank, split_blocks(blocks, level + 1), bits[slot], put)
    for copy in copies[-1:]:
        copy.start()
    for copy in copies:
        copy.wait()


def relabel_kernel(parts, cuts, count, joint, axis, shift, level, blocks, chosen, *rest):
    own, other = rest[:cuts], rest[cuts:2 * cuts]
    spread = rest[-1]
    outs = [[rest[-3].at[offset]] for offset in range(count)] if joint else [[ref] for ref in rest[-1 - count:-1]]
    if joint:
        outs[1 % count].append(rest[-2])
    width = spread.shape[1] // 2

    def put(first, size, value):
        spread[first:first + size] = jnp.concatenate(split2(value), axis=1)

    cross_level(
        put, axis, shift, blocks, level,
        lambda first, size: unpack(own, first, size, parts),
        lambda first, size: unpack(other, first, size, parts),
    )
    piece_rows = spread.shape[0] // (2 * count)
    for index, targets in enumerate(outs):
        for side in range(2):
            place = (index * 2 + side) * piece_rows
            out = jnp.dot(chosen[place:place + piece_rows], spread[...], preferred_element_type=F32)
            out = out[:, :width] + out[:, width:]
            for target in targets:
                pack(target.at[side, :piece_rows // parts], out, parts)


def gather_kernel(parts, count, picks, axis, level, slot, bits, blocks, *rest):
    received, outs = rest[:count], rest[-3 - CORE_SPLIT:-3]
    both, before, after = rest[-3:]
    me = lax.axis_index(axis)
    rows, width = both.shape[1:]
    piece_rows = rows // count
    run = piece_rows // parts
    for offset, ref in enumerate(received):
        ref = ref if picks[offset] is None else ref.at[picks[offset]]
        start = pl.multiple_of(jnp.bitwise_xor(me, offset) * piece_rows, piece_rows)
        for side in range(2):
            for part in range(parts):
                both[side, pl.ds(start + part * run, run), :] = ref[
                    side, :run, part * width:(part + 1) * width
                ]
    nodes, rank = blocks.shape[1], blocks.shape[2] // 2
    for node in range(nodes):
        span = slice(node * rank, (node + 1) * rank)
        before[span] = product(
            blocks[level, node], jnp.concatenate([both[0, span], both[1, span]], axis=0)
        )
    packed_level(before, blocks, level + 1, bits[slot], outs, after, parts)


SMEM = pl.BlockSpec(memory_space=pltpu.SMEM)
VMEM = pl.BlockSpec(memory_space=pltpu.VMEM)
HBM = pl.BlockSpec(memory_space=pltpu.HBM)
ANY = pl.BlockSpec(memory_space=pl.ANY)


def on_device(coefficients, transfer, local_bits, relabel):
    levels = transfer.shape[0]
    nodes, rank, columns = coefficients.shape
    rows = nodes * rank
    n_src, n_tgt = lax.axis_size("src"), lax.axis_size("tgt")
    src_far, tgt_far = n_src // 2, n_tgt // 2
    shape = jax.ShapeDtypeStruct
    chunks = [(group, part, parts) for group, parts in enumerate(CUTS) for part in range(parts)]
    store = {}

    def run(kernel, out_shape, in_specs, out_specs, scratch, args, aliases=None, limit=VMEM_LIMIT):
        extra = [store["token"]] if "token" in store else []
        out = pl.pallas_call(
            kernel,
            out_shape=out_shape,
            in_specs=list(in_specs) + [ANY] * len(extra),
            out_specs=out_specs,
            scratch_shapes=scratch,
            input_output_aliases=aliases or {},
            compiler_params=pltpu.CompilerParams(vmem_limit_bytes=limit),
            cost_estimate=pl.CostEstimate(flops=0, bytes_accessed=0, transcendentals=0),
        )(*args, *extra)
        store["token"] = out[0]
        return out

    def packed(parts, count=1):
        return [shape((rows // parts // count, GROUP), F32)] * count

    def narrow(parts, count):
        return [pltpu.VMEM((rows, GROUP // parts), F32)] * count

    def step_a(index):
        wanted = chunks[1:] if index else chunks[:1]
        groups = wanted[-1][0] - wanted[0][0] + 1
        out = run(
            functools.partial(first_kernel, tuple(wanted)),
            [shape((rows // parts + PAD, GROUP), F32) for _, _, parts in wanted],
            [SMEM, HBM, HBM],
            [VMEM] * len(wanted),
            [
                pltpu.VMEM((nodes, rank, groups * GROUP), F32),
                pltpu.VMEM(transfer.shape[1:], F32),
                pltpu.VMEM((rows, GROUP), F32),
                pltpu.SemaphoreType.DMA((2,)),
            ],
            [local_bits, coefficients, transfer],
            limit=FIRST_LIMIT,
        )
        for offset, array in enumerate(out):
            store["whole", index + offset] = array
        if not index or LAG[1] == 2:
            store["far", index] = partner_2(out[0], "src", src_far)

    def step_p(_):
        ends = STAGES[1:] + (levels,)
        blocks = run(
            prepare_kernel,
            [shape((end - first, nodes, 2 * rank, 2 * rank), BF16) for first, end in zip(STAGES, ends)],
            [HBM],
            [VMEM] * len(STAGES),
            [pltpu.VMEM((levels - 1,) + transfer.shape[1:], F32), pltpu.SemaphoreType.DMA((levels - 1,))],
            [transfer],
        )
        for first, array in zip(STAGES, blocks):
            store["blocks", first] = array

    def step_q(_):
        store["chosen"] = run(
            functools.partial(choose_kernel, "tgt"),
            [shape((rows, rows), BF16)],
            [VMEM],
            [VMEM],
            [],
            [relabel.reshape(rows, 1)],
        )[0]

    def step_r(index):
        array = store["whole", index]
        array = run(
            release_kernel,
            [shape(array.shape, F32)],
            [ANY, ANY],
            [ANY],
            [],
            [array, store["far", index - LAG[index]]],
            aliases={0: 0},
        )[0]
        store["whole", index] = array
        store["far", index] = partner_2(array, "src", src_far)

    def step_b(index):
        _, _, parts = chunks[index]
        cuts = Y_CUTS[index]
        ended = []
        own = run(
            functools.partial(pair_kernel, parts, cuts, "src", src_far.bit_length() - 1, 0, 1),
            packed(parts, cuts),
            [SMEM, VMEM, VMEM, VMEM] + [ANY] * len(ended),
            [VMEM] * cuts,
            narrow(parts, 2),
            [local_bits, store["blocks", 1], store["whole", index], store["far", index], *ended],
        )
        store["own", index] = own
        store["near", index] = [partner_2(piece, "src", 1) for piece in own]

    def step_c(index):
        _, _, parts = chunks[index]
        cuts = Y_CUTS[index]
        joint = index < JOINT
        piece = (2, rows // n_tgt // parts, GROUP)
        pieces = run(
            functools.partial(relabel_kernel, parts, cuts, tgt_far, joint, "src", 0, 0),
            [shape((tgt_far, 2, piece[1] + PAD_X, GROUP), F32), shape(piece, F32)] if joint else [shape(piece, F32)] * tgt_far,
            [VMEM] * (2 + 2 * cuts),
            [VMEM] * (2 if joint else tgt_far),
            [pltpu.VMEM((rows, 2 * GROUP // parts), BF16)],
            [store["blocks", 3], store["chosen"], *store["own", index], *store["near", index]],
        )
        for offset, piece in enumerate(pieces):
            store["piece", index, offset] = piece

    def step_t(index):
        store["moved", index, 1] = partner_2(store["piece", index, 1 % tgt_far], "tgt", 1)

    def step_x(index):
        if index >= JOINT:
            for offset in range(2, n_tgt):
                store["moved", index, offset] = partner_2(
                    store["piece", index, offset % tgt_far], "tgt", offset
                )
            return
        joint = store["piece", index, 0]
        for offset in range(2, n_tgt, 2):
            first = offset % tgt_far
            both = joint if tgt_far == 2 else joint[first:first + 2]
            store["moved", index, offset] = partner_2(both, "tgt", offset)

    def step_s(index):
        if index < JOINT:
            for offset in range(2, n_tgt, 2):
                joint = store["moved", index, offset]
                cross = run(cross_kernel, [shape(joint.shape[1:], F32)], [VMEM], [VMEM], [], [joint])[0]
                store["moved", index, offset + 1] = partner_2(cross, "tgt", 1)

    def step_d(index):
        _, _, parts = chunks[index]
        joint = index < JOINT
        picks = tuple(0 if joint and offset % 2 == 0 else None for offset in range(n_tgt))
        store["mid", index] = run(
            functools.partial(gather_kernel, parts, n_tgt, picks, "tgt", 0, 2),
            packed(parts, CORE_SPLIT),
            [SMEM, VMEM] + [VMEM] * n_tgt,
            [VMEM] * CORE_SPLIT,
            [pltpu.VMEM((2, rows, GROUP // parts), F32)] + narrow(parts, 2),
            [
                local_bits, store["blocks", 4], store["piece", index, 0],
                *(store["moved", index, offset] for offset in range(1, n_tgt)),
            ],
        )
        store["core", index] = [partner_2(piece, "tgt", 1) for piece in store["mid", index]]

    def step_e(index):
        group, part, parts = chunks[index]
        final = index == len(chunks) - 1
        earlier = [store["out", index - 1]] if part else []
        if final:
            earlier += [store["out", chunks.index((at, count - 1, count))] for at, count in enumerate(CUTS[:-1])]
        store["out", index] = run(
            functools.partial(last_kernel, parts, part, len(CUTS) - 1 if final else 0, "tgt", 0, 0, 3),
            [shape((nodes, rank, columns) if final else (rows, GROUP), F32)],
            [SMEM, VMEM] + [VMEM] * (2 * CORE_SPLIT + len(earlier)),
            [HBM if final else VMEM],
            narrow(parts, 1) + [pltpu.VMEM((rows, GROUP), F32), pltpu.SemaphoreType.DMA((len(CUTS),))],
            [local_bits, store["blocks", 6], *store["mid", index], *store["core", index], *earlier],
        )[0]

    steps = {
        "A": step_a, "P": step_p, "Q": step_q, "R": step_r,
        "B": step_b, "C": step_c, "T": step_t, "X": step_x, "S": step_s, "D": step_d, "E": step_e,
    }

    def follow(names):
        for name in names:
            steps[name[0]](int(name[1:]))

    kept = ("piece", "moved", "out")

    def apart(names):
        def work():
            before = dict(store)
            follow(names)
            made = {key: value for key, value in store.items() if before.get(key) is not value and key[0] in kept}
            keys.extend(key for key in made if key not in keys)
            store.clear()
            store.update(before)
            return list(made.values())

        keys = []
        shapes = jax.eval_shape(work)
        made = lax.cond(
            local_bits[0] >= 0, work, lambda: jax.tree.map(lambda x: jnp.zeros(x.shape, x.dtype), shapes)
        )
        store.update(zip(keys, made))
        store["token"] = made[0]

    for names in ORDER:
        if isinstance(names, str):
            follow([names])
        else:
            apart(names)
    return store["out", len(chunks) - 1]


ORDER = (
    'A0',
    'A1',
    'P0',
    'Q0',
    'B0',
    'R2',
    'R3',
    'B1',
    'C0',
    'T0',
    'X0',
    'B2',
    'C1',
    'T1',
    'X1',
    'S0',
    'D0',
    'C2',
    'T2',
    'X2',
    'B3',
    'S1',
    'D1',
    'S2',
    'C3',
    'T3',
    'X3',
    'D2',
    'E0',
    'E1',
    'S3',
    'D3',
    'E2',
    'E3',
)


def solution(mesh):
    placed = (P(("src", "tgt"), None, None), P(None, ("src", "tgt"), None, None), P(), P())
    return jax.shard_map(
        on_device,
        mesh=mesh,
        in_specs=placed,
        out_specs=P(("src", "tgt"), None, None),
        check_vma=False,
    )
```

```python
import functools

import jax
import jax.numpy as jnp
from jax import lax
from jax.experimental import pallas as pl
from jax.experimental.pallas import tpu as pltpu
from jax.sharding import PartitionSpec as P

F32, BF16 = jnp.float32, jnp.bfloat16
GROUP = 128
CUTS = (1, 1, 1, 1)
PAD = 8
PAD_X = 0
LAG = (0, 2, 2, 2)
CORE_SPLIT = 1
Y_CUTS = (2, 2, 2, 1)
JOINT = (1, 1, 1, 0)
STAGES = (1, 3, 4, 6)
VMEM_LIMIT = 16 * 1024 * 1024
FIRST_LIMIT = 62 * 1024 * 1024


def partner_2(shard, axis, mask):
    return lax.ppermute(shard, axis, [(i, i ^ mask) for i in range(lax.axis_size(axis))])


def split2(x):
    high = x.astype(BF16)
    return high, (x - high.astype(F32)).astype(BF16)


def product(blocks, x):
    half, width = blocks.shape[0] // 2, x.shape[1]
    out = jnp.dot(blocks, jnp.concatenate(split2(x), axis=1), preferred_element_type=F32)
    return (out[:half, :width] + out[:half, width:]) + (out[half:, :width] + out[half:, width:])


def unpack(refs, first, count, parts, extra=0):
    each = refs[0].shape[0] - extra
    width = refs[0].shape[1] // parts
    run = each * len(refs)
    lane = first // run * width
    place = first % run
    return refs[place // each][place % each:place % each + count, lane:lane + width]


def pack(out_ref, rows, parts):
    run = out_ref.shape[0]
    out_ref[...] = jnp.concatenate([rows[part * run:(part + 1) * run, :] for part in range(parts)], axis=1)


def local_level(state, rank, blocks, bit, put, lanes=slice(None)):
    nodes = state.shape[0] // rank
    for index in range(nodes // 2):
        low_bits = jnp.bitwise_and(index, jnp.left_shift(1, bit) - 1)
        low = jnp.left_shift(jnp.right_shift(index, bit), bit + 1) | low_bits
        high = low | jnp.left_shift(1, bit)
        spans = [pl.ds(pl.multiple_of(node * rank, rank), rank) for node in (low, high)]
        both = jnp.concatenate([state[span, lanes] for span in spans], axis=0)
        out = product(blocks(low, high), both)
        put(spans[0], out[:rank])
        put(spans[1], out[rank:])


def split_blocks(ref, level):
    rank = ref.shape[2] // 2

    def blocks(low, high):
        return jnp.concatenate(
            [ref[level, low, :rank], ref[level, high, :rank], ref[level, low, rank:], ref[level, high, rank:]],
            axis=0,
        )

    return blocks


def packed_level(state, blocks, level, bit, outs, after, parts):
    rank = blocks.shape[2] // 2
    target = outs[0] if parts == 1 and len(outs) == 1 else after

    def put(span, value):
        target[span, :] = value

    local_level(state, rank, split_blocks(blocks, level), bit, put)
    if target is after:
        each = outs[0].shape[0]
        run = each * len(outs)
        for index, out_ref in enumerate(outs):
            row = [after[part * run + index * each:part * run + (index + 1) * each] for part in range(parts)]
            out_ref[...] = row[0] if parts == 1 else jnp.concatenate(row, axis=1)


def first_kernel(chunks, bits, x_hbm, g_hbm, *rest):
    outs, (x_ref, g_ref, after, arrived) = rest[-4 - len(chunks):-4], rest[-4:]
    nodes, rank, _ = x_ref.shape
    lanes = outs[0].shape[1]
    first, groups = chunks[0][0], x_ref.shape[2] // lanes
    x_copy = pltpu.make_async_copy(
        x_hbm.at[:, :, first * lanes:(first + groups) * lanes], x_ref, arrived.at[0]
    )
    g_copy = pltpu.make_async_copy(g_hbm.at[0], g_ref, arrived.at[1])
    x_copy.start()
    g_copy.start()
    x_copy.wait()
    g_copy.wait()
    state = x_ref.reshape(nodes * rank, x_ref.shape[2])

    def blocks(low, high):
        top = jnp.concatenate([g_ref[low], g_ref[high]], axis=0)
        return jnp.concatenate(split2(top), axis=0)

    bit = bits(0)
    for (group, part, parts), out_ref in zip(chunks, outs):
        width = lanes // parts
        begin = (group - first) * lanes + part * width
        run = out_ref.shape[0] - PAD

        def put(span, value):
            if parts == 1:
                out_ref[span, :] = value
            else:
                after[span, :width] = value

        local_level(state, rank, blocks, bit, put, slice(begin, begin + width))
        if parts > 1:
            out_ref[:run, :] = jnp.concatenate(
                [after[at * run:(at + 1) * run, :width] for at in range(parts)], axis=1
            )
        out_ref[run:, :] = jnp.zeros((PAD, lanes), F32)


def release_kernel(*_):
    pass


def cross_kernel(joint, *rest):
    rest[-1][...] = joint[1]


def prepare_kernel(g_hbm, *rest):
    outs, (g_ref, arrived) = rest[-2 - len(STAGES):-2], rest[-2:]
    levels, nodes, rank, _ = g_ref.shape
    copies = [
        pltpu.make_async_copy(g_hbm.at[level + 1], g_ref.at[level], arrived.at[level])
        for level in range(levels)
    ]
    for copy in copies:
        copy.start()
    for first, out_ref in zip(STAGES, outs):
        for offset in range(out_ref.shape[0]):
            level = first - 1 + offset
            copies[level].wait()

            def split(node, carry):
                high, low = split2(g_ref[level, node])
                out_ref[offset, node, :rank] = high
                out_ref[offset, node, rank:] = low
                return carry

            lax.fori_loop(0, nodes, split, 0)


def choose_kernel(axis, relabel_ref, *rest):
    out_ref = rest[-1]
    rows = out_ref.shape[0]
    count = lax.axis_size(axis)
    half, piece_rows = count // 2, rows // count
    group = lax.axis_index(axis) % half
    for offset in range(half):
        for side in range(2):
            piece = side * half + jnp.bitwise_xor(group, offset)
            start = pl.multiple_of(piece * piece_rows, piece_rows)
            wanted = relabel_ref[pl.ds(start, piece_rows), :]
            column = lax.broadcasted_iota(jnp.int32, (piece_rows, rows), 1)
            place = (offset * 2 + side) * piece_rows
            out_ref[place:place + piece_rows, :] = jnp.where(wanted == column, 1.0, 0.0).astype(BF16)


def cross_level(put, axis, shift, blocks, level, take_own, take_other):
    upper = jnp.bitwise_and(jnp.right_shift(lax.axis_index(axis), shift), 1) == 1
    nodes, rank = blocks.shape[1], blocks.shape[2] // 2
    for node in range(nodes):
        own, other = take_own(node * rank, rank), take_other(node * rank, rank)
        leading = jnp.where(upper, other, own)
        trailing = jnp.where(upper, own, other)
        value = product(blocks[level, node], jnp.concatenate([leading, trailing], axis=0))
        put(node * rank, rank, value)


def with_bits(kernel):
    def body(bits_hbm, *refs):
        *refs, bits_ref, arrived = refs
        copy = pltpu.make_async_copy(bits_hbm, bits_ref, arrived)
        copy.start()

        def bits(slot):
            copy.wait()
            return bits_ref[slot]

        kernel(bits, *refs)

    return body


def put_rows(ref):
    def put(first, count, value):
        ref[first:first + count, :] = value

    return put


def pair_kernel(parts, cuts, axis, shift, level, slot, bits, blocks, own, other, *rest):
    outs, before, after = rest[-2 - cuts:-2], *rest[-2:]
    cross_level(
        put_rows(before), axis, shift, blocks, level,
        lambda first, count: unpack([own], first, count, parts, PAD),
        lambda first, count: unpack([other], first, count, parts, PAD),
    )
    packed_level(before, blocks, level + 1, bits(slot), outs, after, parts)


def last_kernel(parts, part, done, axis, shift, level, slot, bits, blocks, *rest):
    own, other, rest = rest[:CORE_SPLIT], rest[CORE_SPLIT:2 * CORE_SPLIT], rest[2 * CORE_SPLIT:]
    out_ref, before, after, sent = rest[-4:]
    nodes, rank = blocks.shape[1], blocks.shape[2] // 2
    width = before.shape[1]
    lanes = after.shape[1]
    earlier = rest[:1] if part else ()
    copies = [
        pltpu.make_async_copy(
            ref.reshape(nodes, rank, lanes), out_ref.at[:, :, at * lanes:(at + 1) * lanes], sent.at[at]
        )
        for at, ref in enumerate([*rest[len(earlier):len(earlier) + done], after] if done else [])
    ]
    for copy in copies[:-1]:
        copy.start()
    cross_level(
        put_rows(before), axis, shift, blocks, level,
        lambda first, count: unpack(own, first, count, parts),
        lambda first, count: unpack(other, first, count, parts),
    )
    target = after if done else out_ref
    for ref in earlier:
        target[...] = ref[...]

    def put(span, value):
        target[span, part * width:(part + 1) * width] = value

    local_level(before, rank, split_blocks(blocks, level + 1), bits(slot), put)
    for copy in copies[-1:]:
        copy.start()
    for copy in copies:
        copy.wait()


def relabel_kernel(parts, cuts, count, joint, axis, shift, level, blocks, chosen, *rest):
    own, other = rest[:cuts], rest[cuts:2 * cuts]
    spread = rest[-1]
    outs = [[rest[-3].at[offset]] for offset in range(count)] if joint else [[ref] for ref in rest[-1 - count:-1]]
    if joint:
        outs[1 % count].append(rest[-2])
    width = spread.shape[1] // 2

    def put(first, size, value):
        spread[first:first + size] = jnp.concatenate(split2(value), axis=1)

    cross_level(
        put, axis, shift, blocks, level,
        lambda first, size: unpack(own, first, size, parts),
        lambda first, size: unpack(other, first, size, parts),
    )
    piece_rows = spread.shape[0] // (2 * count)
    for index, targets in enumerate(outs):
        for side in range(2):
            place = (index * 2 + side) * piece_rows
            out = jnp.dot(chosen[place:place + piece_rows], spread[...], preferred_element_type=F32)
            out = out[:, :width] + out[:, width:]
            for target in targets:
                pack(target.at[side, :piece_rows // parts], out, parts)


def gather_kernel(parts, count, picks, axis, level, slot, bits, blocks, *rest):
    received, outs = rest[:count], rest[-3 - CORE_SPLIT:-3]
    both, before, after = rest[-3:]
    me = lax.axis_index(axis)
    rows, width = both.shape[1:]
    piece_rows = rows // count
    run = piece_rows // parts
    for offset, ref in enumerate(received):
        ref = ref if picks[offset] is None else ref.at[picks[offset]]
        start = pl.multiple_of(jnp.bitwise_xor(me, offset) * piece_rows, piece_rows)
        for side in range(2):
            for part in range(parts):
                both[side, pl.ds(start + part * run, run), :] = ref[
                    side, :run, part * width:(part + 1) * width
                ]
    nodes, rank = blocks.shape[1], blocks.shape[2] // 2
    for node in range(nodes):
        span = slice(node * rank, (node + 1) * rank)
        before[span] = product(
            blocks[level, node], jnp.concatenate([both[0, span], both[1, span]], axis=0)
        )
    packed_level(before, blocks, level + 1, bits(slot), outs, after, parts)


VMEM = pl.BlockSpec(memory_space=pltpu.VMEM)
HBM = pl.BlockSpec(memory_space=pltpu.HBM)
ANY = pl.BlockSpec(memory_space=pl.ANY)


def on_device(coefficients, transfer, local_bits, relabel):
    levels = transfer.shape[0]
    nodes, rank, columns = coefficients.shape
    rows = nodes * rank
    n_src, n_tgt = lax.axis_size("src"), lax.axis_size("tgt")
    src_far, tgt_far = n_src // 2, n_tgt // 2
    shape = jax.ShapeDtypeStruct
    chunks = [(group, part, parts) for group, parts in enumerate(CUTS) for part in range(parts)]
    store = {}

    def run(kernel, out_shape, in_specs, out_specs, scratch, args, aliases=None, limit=VMEM_LIMIT):
        extra = [store["token"]] if "token" in store else []
        if args[0] is local_bits:
            kernel = with_bits(kernel)
            scratch = [*scratch, pltpu.SMEM(local_bits.shape, jnp.int32), pltpu.SemaphoreType.DMA]
        out = pl.pallas_call(
            kernel,
            out_shape=out_shape,
            in_specs=list(in_specs) + [ANY] * len(extra),
            out_specs=out_specs,
            scratch_shapes=scratch,
            input_output_aliases=aliases or {},
            compiler_params=pltpu.CompilerParams(vmem_limit_bytes=limit),
            cost_estimate=pl.CostEstimate(flops=0, bytes_accessed=0, transcendentals=0),
        )(*args, *extra)
        store["token"] = out[0]
        return out

    def packed(parts, count=1):
        return [shape((rows // parts // count, GROUP), F32)] * count

    def narrow(parts, count):
        return [pltpu.VMEM((rows, GROUP // parts), F32)] * count

    def step_a(index):
        wanted = chunks[1:] if index else chunks[:1]
        groups = wanted[-1][0] - wanted[0][0] + 1
        out = run(
            functools.partial(first_kernel, tuple(wanted)),
            [shape((rows // parts + PAD, GROUP), F32) for _, _, parts in wanted],
            [HBM, HBM, HBM],
            [VMEM] * len(wanted),
            [
                pltpu.VMEM((nodes, rank, groups * GROUP), F32),
                pltpu.VMEM(transfer.shape[1:], F32),
                pltpu.VMEM((rows, GROUP), F32),
                pltpu.SemaphoreType.DMA((2,)),
            ],
            [local_bits, coefficients, transfer],
            limit=FIRST_LIMIT,
        )
        for offset, array in enumerate(out):
            store["whole", index + offset] = array
        if not index or LAG[1] == 2:
            store["far", index] = partner_2(out[0], "src", src_far)

    def step_p(_):
        ends = STAGES[1:] + (levels,)
        blocks = run(
            prepare_kernel,
            [shape((end - first, nodes, 2 * rank, 2 * rank), BF16) for first, end in zip(STAGES, ends)],
            [HBM],
            [VMEM] * len(STAGES),
            [pltpu.VMEM((levels - 1,) + transfer.shape[1:], F32), pltpu.SemaphoreType.DMA((levels - 1,))],
            [transfer],
        )
        for first, array in zip(STAGES, blocks):
            store["blocks", first] = array

    def step_q(_):
        store["chosen"] = run(
            functools.partial(choose_kernel, "tgt"),
            [shape((rows, rows), BF16)],
            [VMEM],
            [VMEM],
            [],
            [relabel.reshape(rows, 1)],
        )[0]

    def step_r(index):
        array = store["whole", index]
        array = run(
            release_kernel,
            [shape(array.shape, F32)],
            [ANY, ANY],
            [ANY],
            [],
            [array, store["far", index - LAG[index]]],
            aliases={0: 0},
        )[0]
        store["whole", index] = array
        store["far", index] = partner_2(array, "src", src_far)

    def step_b(index):
        _, _, parts = chunks[index]
        cuts = Y_CUTS[index]
        ended = []
        own = run(
            functools.partial(pair_kernel, parts, cuts, "src", src_far.bit_length() - 1, 0, 1),
            packed(parts, cuts),
            [HBM, VMEM, VMEM, VMEM] + [ANY] * len(ended),
            [VMEM] * cuts,
            narrow(parts, 2),
            [local_bits, store["blocks", 1], store["whole", index], store["far", index], *ended],
        )
        store["own", index] = own
        store["near", index] = [partner_2(piece, "src", 1) for piece in own]

    def step_c(index):
        _, _, parts = chunks[index]
        cuts = Y_CUTS[index]
        joint = JOINT[index]
        piece = (2, rows // n_tgt // parts, GROUP)
        pieces = run(
            functools.partial(relabel_kernel, parts, cuts, tgt_far, bool(joint), "src", 0, 0),
            [shape((tgt_far, 2, piece[1] + PAD_X, GROUP), F32), shape(piece, F32)] if joint else [shape(piece, F32)] * tgt_far,
            [VMEM] * (2 + 2 * cuts),
            [VMEM] * (2 if joint else tgt_far),
            [pltpu.VMEM((rows, 2 * GROUP // parts), BF16)],
            [store["blocks", 3], store["chosen"], *store["own", index], *store["near", index]],
        )
        for offset, piece in enumerate(pieces):
            store["piece", index, offset] = piece

    def step_t(index):
        store["moved", index, 1] = partner_2(store["piece", index, 1 % tgt_far], "tgt", 1)

    def step_x(index):
        if not JOINT[index]:
            for offset in range(2, n_tgt):
                store["moved", index, offset] = partner_2(
                    store["piece", index, offset % tgt_far], "tgt", offset
                )
            return
        joint = store["piece", index, 0]
        for offset in range(2, n_tgt, 2):
            first = offset % tgt_far
            both = joint if tgt_far == 2 else joint[first:first + 2]
            store["moved", index, offset] = partner_2(both, "tgt", offset)

    def step_s(index):
        if JOINT[index]:
            for offset in range(2, n_tgt, 2):
                joint = store["moved", index, offset]
                cross = run(cross_kernel, [shape(joint.shape[1:], F32)], [VMEM], [VMEM], [], [joint])[0]
                store["moved", index, offset + 1] = partner_2(cross, "tgt", 1)

    def step_d(index):
        _, _, parts = chunks[index]
        joint = JOINT[index]
        picks = tuple(0 if joint and offset % 2 == 0 else None for offset in range(n_tgt))
        store["mid", index] = run(
            functools.partial(gather_kernel, parts, n_tgt, picks, "tgt", 0, 2),
            packed(parts, CORE_SPLIT),
            [HBM, VMEM] + [VMEM] * n_tgt,
            [VMEM] * CORE_SPLIT,
            [pltpu.VMEM((2, rows, GROUP // parts), F32)] + narrow(parts, 2),
            [
                local_bits, store["blocks", 4], store["piece", index, 0],
                *(store["moved", index, offset] for offset in range(1, n_tgt)),
            ],
        )
        store["core", index] = [partner_2(piece, "tgt", 1) for piece in store["mid", index]]

    def step_e(index):
        group, part, parts = chunks[index]
        final = index == len(chunks) - 1
        earlier = [store["out", index - 1]] if part else []
        if final:
            earlier += [store["out", chunks.index((at, count - 1, count))] for at, count in enumerate(CUTS[:-1])]
        store["out", index] = run(
            functools.partial(last_kernel, parts, part, len(CUTS) - 1 if final else 0, "tgt", 0, 0, 3),
            [shape((nodes, rank, columns) if final else (rows, GROUP), F32)],
            [HBM, VMEM] + [VMEM] * (2 * CORE_SPLIT + len(earlier)),
            [HBM if final else VMEM],
            narrow(parts, 1) + [pltpu.VMEM((rows, GROUP), F32), pltpu.SemaphoreType.DMA((len(CUTS),))],
            [local_bits, store["blocks", 6], *store["mid", index], *store["core", index], *earlier],
        )[0]

    steps = {
        "A": step_a, "P": step_p, "Q": step_q, "R": step_r,
        "B": step_b, "C": step_c, "T": step_t, "X": step_x, "S": step_s, "D": step_d, "E": step_e,
    }

    for name in ORDER:
        steps[name[0]](int(name[1:]))
    return store["out", len(chunks) - 1]


ORDER = (
    'A0',
    'A1',
    'P0',
    'Q0',
    'B0',
    'R2',
    'R3',
    'B1',
    'C0',
    'T0',
    'X0',
    'B2',
    'C1',
    'T1',
    'X1',
    'S0',
    'D0',
    'C2',
    'T2',
    'X2',
    'B3',
    'S1',
    'D1',
    'S2',
    'C3',
    'T3',
    'X3',
    'D2',
    'E0',
    'E1',
    'S3',
    'D3',
    'E2',
    'E3',
)


def solution(mesh):
    placed = (P(("src", "tgt"), None, None), P(None, ("src", "tgt"), None, None), P(), P())
    return jax.shard_map(
        on_device,
        mesh=mesh,
        in_specs=placed,
        out_specs=P(("src", "tgt"), None, None),
        check_vma=False,
    )
```

```python
import functools

import jax
import jax.numpy as jnp
from jax import lax
from jax.experimental import pallas as pl
from jax.experimental.pallas import tpu as pltpu
from jax.sharding import PartitionSpec as P

F32, BF16 = jnp.float32, jnp.bfloat16
GROUP = 128
CUTS = (1, 1, 1, 1)
PAD = 8
PAD_X = 0
LAG = (0, 2, 2, 2)
CORE_SPLIT = 1
Y_CUTS = (1, 2, 2, 1)
JOINT = (1, 1, 1, 0)
STAGES = (1, 3, 4, 6)
VMEM_LIMIT = 16 * 1024 * 1024
FIRST_LIMIT = 62 * 1024 * 1024


def partner_2(shard, axis, mask):
    return lax.ppermute(shard, axis, [(i, i ^ mask) for i in range(lax.axis_size(axis))])


def split2(x):
    high = x.astype(BF16)
    return high, (x - high.astype(F32)).astype(BF16)


def product(blocks, x):
    half, width = blocks.shape[0] // 2, x.shape[1]
    out = jnp.dot(blocks, jnp.concatenate(split2(x), axis=1), preferred_element_type=F32)
    return (out[:half, :width] + out[:half, width:]) + (out[half:, :width] + out[half:, width:])


def unpack(refs, first, count, parts, extra=0):
    each = refs[0].shape[0] - extra
    width = refs[0].shape[1] // parts
    run = each * len(refs)
    lane = first // run * width
    place = first % run
    return refs[place // each][place % each:place % each + count, lane:lane + width]


def pack(out_ref, rows, parts):
    run = out_ref.shape[0]
    out_ref[...] = jnp.concatenate([rows[part * run:(part + 1) * run, :] for part in range(parts)], axis=1)


def local_level(state, rank, blocks, bit, put, lanes=slice(None)):
    nodes = state.shape[0] // rank
    for index in range(nodes // 2):
        low_bits = jnp.bitwise_and(index, jnp.left_shift(1, bit) - 1)
        low = jnp.left_shift(jnp.right_shift(index, bit), bit + 1) | low_bits
        high = low | jnp.left_shift(1, bit)
        spans = [pl.ds(pl.multiple_of(node * rank, rank), rank) for node in (low, high)]
        both = jnp.concatenate([state[span, lanes] for span in spans], axis=0)
        out = product(blocks(low, high), both)
        put(spans[0], out[:rank])
        put(spans[1], out[rank:])


def split_blocks(ref, level):
    rank = ref.shape[2] // 2

    def blocks(low, high):
        return jnp.concatenate(
            [ref[level, low, :rank], ref[level, high, :rank], ref[level, low, rank:], ref[level, high, rank:]],
            axis=0,
        )

    return blocks


def packed_level(state, blocks, level, bit, outs, after, parts):
    rank = blocks.shape[2] // 2
    target = outs[0] if parts == 1 and len(outs) == 1 else after

    def put(span, value):
        target[span, :] = value

    local_level(state, rank, split_blocks(blocks, level), bit, put)
    if target is after:
        each = outs[0].shape[0]
        run = each * len(outs)
        for index, out_ref in enumerate(outs):
            row = [after[part * run + index * each:part * run + (index + 1) * each] for part in range(parts)]
            out_ref[...] = row[0] if parts == 1 else jnp.concatenate(row, axis=1)


def first_kernel(chunks, bits, x_hbm, g_hbm, *rest):
    outs, (x_ref, g_ref, after, arrived) = rest[-4 - len(chunks):-4], rest[-4:]
    nodes, rank, _ = x_ref.shape
    lanes = outs[0].shape[1]
    first, groups = chunks[0][0], x_ref.shape[2] // lanes
    x_copy = pltpu.make_async_copy(
        x_hbm.at[:, :, first * lanes:(first + groups) * lanes], x_ref, arrived.at[0]
    )
    g_copy = pltpu.make_async_copy(g_hbm.at[0], g_ref, arrived.at[1])
    x_copy.start()
    g_copy.start()
    x_copy.wait()
    g_copy.wait()
    state = x_ref.reshape(nodes * rank, x_ref.shape[2])

    def blocks(low, high):
        top = jnp.concatenate([g_ref[low], g_ref[high]], axis=0)
        return jnp.concatenate(split2(top), axis=0)

    bit = bits(0)
    for (group, part, parts), out_ref in zip(chunks, outs):
        width = lanes // parts
        begin = (group - first) * lanes + part * width
        run = out_ref.shape[0] - PAD

        def put(span, value):
            if parts == 1:
                out_ref[span, :] = value
            else:
                after[span, :width] = value

        local_level(state, rank, blocks, bit, put, slice(begin, begin + width))
        if parts > 1:
            out_ref[:run, :] = jnp.concatenate(
                [after[at * run:(at + 1) * run, :width] for at in range(parts)], axis=1
            )
        out_ref[run:, :] = jnp.zeros((PAD, lanes), F32)


def release_kernel(*_):
    pass


def cross_kernel(joint, *rest):
    rest[-1][...] = joint[1]


def prepare_kernel(g_hbm, *rest):
    outs, (g_ref, arrived) = rest[-2 - len(STAGES):-2], rest[-2:]
    levels, nodes, rank, _ = g_ref.shape
    copies = [
        pltpu.make_async_copy(g_hbm.at[level + 1], g_ref.at[level], arrived.at[level])
        for level in range(levels)
    ]
    for copy in copies:
        copy.start()
    for first, out_ref in zip(STAGES, outs):
        for offset in range(out_ref.shape[0]):
            level = first - 1 + offset
            copies[level].wait()

            def split(node, carry):
                high, low = split2(g_ref[level, node])
                out_ref[offset, node, :rank] = high
                out_ref[offset, node, rank:] = low
                return carry

            lax.fori_loop(0, nodes, split, 0)


def choose_kernel(axis, relabel_ref, *rest):
    out_ref = rest[-1]
    rows = out_ref.shape[0]
    count = lax.axis_size(axis)
    half, piece_rows = count // 2, rows // count
    group = lax.axis_index(axis) % half
    for offset in range(half):
        for side in range(2):
            piece = side * half + jnp.bitwise_xor(group, offset)
            start = pl.multiple_of(piece * piece_rows, piece_rows)
            wanted = relabel_ref[pl.ds(start, piece_rows), :]
            column = lax.broadcasted_iota(jnp.int32, (piece_rows, rows), 1)
            place = (offset * 2 + side) * piece_rows
            out_ref[place:place + piece_rows, :] = jnp.where(wanted == column, 1.0, 0.0).astype(BF16)


def cross_level(put, axis, shift, blocks, level, take_own, take_other):
    upper = jnp.bitwise_and(jnp.right_shift(lax.axis_index(axis), shift), 1) == 1
    nodes, rank = blocks.shape[1], blocks.shape[2] // 2
    for node in range(nodes):
        own, other = take_own(node * rank, rank), take_other(node * rank, rank)
        leading = jnp.where(upper, other, own)
        trailing = jnp.where(upper, own, other)
        value = product(blocks[level, node], jnp.concatenate([leading, trailing], axis=0))
        put(node * rank, rank, value)


def with_bits(kernel):
    def body(bits_hbm, *refs):
        *refs, bits_ref, arrived = refs
        copy = pltpu.make_async_copy(bits_hbm, bits_ref, arrived)
        copy.start()

        def bits(slot):
            copy.wait()
            return bits_ref[slot]

        kernel(bits, *refs)

    return body


def put_rows(ref):
    def put(first, count, value):
        ref[first:first + count, :] = value

    return put


def pair_kernel(parts, cuts, axis, shift, level, slot, bits, blocks, own, other, *rest):
    outs, before, after = rest[-2 - cuts:-2], *rest[-2:]
    cross_level(
        put_rows(before), axis, shift, blocks, level,
        lambda first, count: unpack([own], first, count, parts, PAD),
        lambda first, count: unpack([other], first, count, parts, PAD),
    )
    packed_level(before, blocks, level + 1, bits(slot), outs, after, parts)


def last_kernel(parts, part, done, axis, shift, level, slot, bits, blocks, *rest):
    own, other, rest = rest[:CORE_SPLIT], rest[CORE_SPLIT:2 * CORE_SPLIT], rest[2 * CORE_SPLIT:]
    out_ref, before, after, sent = rest[-4:]
    nodes, rank = blocks.shape[1], blocks.shape[2] // 2
    width = before.shape[1]
    lanes = after.shape[1]
    earlier = rest[:1] if part else ()
    copies = [
        pltpu.make_async_copy(
            ref.reshape(nodes, rank, lanes), out_ref.at[:, :, at * lanes:(at + 1) * lanes], sent.at[at]
        )
        for at, ref in enumerate([*rest[len(earlier):len(earlier) + done], after] if done else [])
    ]
    for copy in copies[:-1]:
        copy.start()
    cross_level(
        put_rows(before), axis, shift, blocks, level,
        lambda first, count: unpack(own, first, count, parts),
        lambda first, count: unpack(other, first, count, parts),
    )
    target = after if done else out_ref
    for ref in earlier:
        target[...] = ref[...]

    def put(span, value):
        target[span, part * width:(part + 1) * width] = value

    local_level(before, rank, split_blocks(blocks, level + 1), bits(slot), put)
    for copy in copies[-1:]:
        copy.start()
    for copy in copies:
        copy.wait()


def relabel_kernel(parts, cuts, count, joint, axis, shift, level, blocks, chosen, *rest):
    own, other = rest[:cuts], rest[cuts:2 * cuts]
    spread = rest[-1]
    outs = [[rest[-3].at[offset]] for offset in range(count)] if joint else [[ref] for ref in rest[-1 - count:-1]]
    if joint:
        outs[1 % count].append(rest[-2])
    width = spread.shape[1] // 2

    def put(first, size, value):
        spread[first:first + size] = jnp.concatenate(split2(value), axis=1)

    cross_level(
        put, axis, shift, blocks, level,
        lambda first, size: unpack(own, first, size, parts),
        lambda first, size: unpack(other, first, size, parts),
    )
    piece_rows = spread.shape[0] // (2 * count)
    for index, targets in enumerate(outs):
        for side in range(2):
            place = (index * 2 + side) * piece_rows
            out = jnp.dot(chosen[place:place + piece_rows], spread[...], preferred_element_type=F32)
            out = out[:, :width] + out[:, width:]
            for target in targets:
                pack(target.at[side, :piece_rows // parts], out, parts)


def gather_kernel(parts, count, picks, axis, level, slot, bits, blocks, *rest):
    received, outs = rest[:count], rest[-3 - CORE_SPLIT:-3]
    both, before, after = rest[-3:]
    me = lax.axis_index(axis)
    rows, width = both.shape[1:]
    piece_rows = rows // count
    run = piece_rows // parts
    for offset, ref in enumerate(received):
        ref = ref if picks[offset] is None else ref.at[picks[offset]]
        start = pl.multiple_of(jnp.bitwise_xor(me, offset) * piece_rows, piece_rows)
        for side in range(2):
            for part in range(parts):
                both[side, pl.ds(start + part * run, run), :] = ref[
                    side, :run, part * width:(part + 1) * width
                ]
    nodes, rank = blocks.shape[1], blocks.shape[2] // 2
    for node in range(nodes):
        span = slice(node * rank, (node + 1) * rank)
        before[span] = product(
            blocks[level, node], jnp.concatenate([both[0, span], both[1, span]], axis=0)
        )
    packed_level(before, blocks, level + 1, bits(slot), outs, after, parts)


VMEM = pl.BlockSpec(memory_space=pltpu.VMEM)
HBM = pl.BlockSpec(memory_space=pltpu.HBM)
ANY = pl.BlockSpec(memory_space=pl.ANY)


def on_device(coefficients, transfer, local_bits, relabel):
    levels = transfer.shape[0]
    nodes, rank, columns = coefficients.shape
    rows = nodes * rank
    n_src, n_tgt = lax.axis_size("src"), lax.axis_size("tgt")
    src_far, tgt_far = n_src // 2, n_tgt // 2
    shape = jax.ShapeDtypeStruct
    chunks = [(group, part, parts) for group, parts in enumerate(CUTS) for part in range(parts)]
    store = {}

    def run(kernel, out_shape, in_specs, out_specs, scratch, args, aliases=None, limit=VMEM_LIMIT):
        extra = [store["token"]] if "token" in store else []
        if args[0] is local_bits:
            kernel = with_bits(kernel)
            scratch = [*scratch, pltpu.SMEM(local_bits.shape, jnp.int32), pltpu.SemaphoreType.DMA]
        out = pl.pallas_call(
            kernel,
            out_shape=out_shape,
            in_specs=list(in_specs) + [ANY] * len(extra),
            out_specs=out_specs,
            scratch_shapes=scratch,
            input_output_aliases=aliases or {},
            compiler_params=pltpu.CompilerParams(vmem_limit_bytes=limit),
            cost_estimate=pl.CostEstimate(flops=0, bytes_accessed=0, transcendentals=0),
        )(*args, *extra)
        store["token"] = out[0]
        return out

    def packed(parts, count=1):
        return [shape((rows // parts // count, GROUP), F32)] * count

    def narrow(parts, count):
        return [pltpu.VMEM((rows, GROUP // parts), F32)] * count

    def step_a(index):
        wanted = chunks[1:] if index else chunks[:1]
        groups = wanted[-1][0] - wanted[0][0] + 1
        out = run(
            functools.partial(first_kernel, tuple(wanted)),
            [shape((rows // parts + PAD, GROUP), F32) for _, _, parts in wanted],
            [HBM, HBM, HBM],
            [VMEM] * len(wanted),
            [
                pltpu.VMEM((nodes, rank, groups * GROUP), F32),
                pltpu.VMEM(transfer.shape[1:], F32),
                pltpu.VMEM((rows, GROUP), F32),
                pltpu.SemaphoreType.DMA((2,)),
            ],
            [local_bits, coefficients, transfer],
            limit=FIRST_LIMIT,
        )
        for offset, array in enumerate(out):
            store["whole", index + offset] = array
        if not index or LAG[1] == 2:
            store["far", index] = partner_2(out[0], "src", src_far)

    def step_p(_):
        ends = STAGES[1:] + (levels,)
        blocks = run(
            prepare_kernel,
            [shape((end - first, nodes, 2 * rank, 2 * rank), BF16) for first, end in zip(STAGES, ends)],
            [HBM],
            [VMEM] * len(STAGES),
            [pltpu.VMEM((levels - 1,) + transfer.shape[1:], F32), pltpu.SemaphoreType.DMA((levels - 1,))],
            [transfer],
        )
        for first, array in zip(STAGES, blocks):
            store["blocks", first] = array

    def step_q(_):
        store["chosen"] = run(
            functools.partial(choose_kernel, "tgt"),
            [shape((rows, rows), BF16)],
            [VMEM],
            [VMEM],
            [],
            [relabel.reshape(rows, 1)],
        )[0]

    def step_r(index):
        array = store["whole", index]
        array = run(
            release_kernel,
            [shape(array.shape, F32)],
            [ANY, ANY],
            [ANY],
            [],
            [array, store["far", index - LAG[index]]],
            aliases={0: 0},
        )[0]
        store["whole", index] = array
        store["far", index] = partner_2(array, "src", src_far)

    def step_b(index):
        _, _, parts = chunks[index]
        cuts = Y_CUTS[index]
        ended = []
        own = run(
            functools.partial(pair_kernel, parts, cuts, "src", src_far.bit_length() - 1, 0, 1),
            packed(parts, cuts),
            [HBM, VMEM, VMEM, VMEM] + [ANY] * len(ended),
            [VMEM] * cuts,
            narrow(parts, 2),
            [local_bits, store["blocks", 1], store["whole", index], store["far", index], *ended],
        )
        store["own", index] = own
        store["near", index] = [partner_2(piece, "src", 1) for piece in own]

    def step_c(index):
        _, _, parts = chunks[index]
        cuts = Y_CUTS[index]
        joint = JOINT[index]
        piece = (2, rows // n_tgt // parts, GROUP)
        pieces = run(
            functools.partial(relabel_kernel, parts, cuts, tgt_far, bool(joint), "src", 0, 0),
            [shape((tgt_far, 2, piece[1] + PAD_X, GROUP), F32), shape(piece, F32)] if joint else [shape(piece, F32)] * tgt_far,
            [VMEM] * (2 + 2 * cuts),
            [VMEM] * (2 if joint else tgt_far),
            [pltpu.VMEM((rows, 2 * GROUP // parts), BF16)],
            [store["blocks", 3], store["chosen"], *store["own", index], *store["near", index]],
        )
        for offset, piece in enumerate(pieces):
            store["piece", index, offset] = piece

    def step_t(index):
        store["moved", index, 1] = partner_2(store["piece", index, 1 % tgt_far], "tgt", 1)

    def step_x(index):
        if not JOINT[index]:
            for offset in range(2, n_tgt):
                store["moved", index, offset] = partner_2(
                    store["piece", index, offset % tgt_far], "tgt", offset
                )
            return
        joint = store["piece", index, 0]
        for offset in range(2, n_tgt, 2):
            first = offset % tgt_far
            both = joint if tgt_far == 2 else joint[first:first + 2]
            store["moved", index, offset] = partner_2(both, "tgt", offset)

    def step_s(index):
        if JOINT[index]:
            for offset in range(2, n_tgt, 2):
                joint = store["moved", index, offset]
                cross = run(cross_kernel, [shape(joint.shape[1:], F32)], [VMEM], [VMEM], [], [joint])[0]
                store["moved", index, offset + 1] = partner_2(cross, "tgt", 1)

    def step_d(index):
        _, _, parts = chunks[index]
        joint = JOINT[index]
        picks = tuple(0 if joint and offset % 2 == 0 else None for offset in range(n_tgt))
        store["mid", index] = run(
            functools.partial(gather_kernel, parts, n_tgt, picks, "tgt", 0, 2),
            packed(parts, CORE_SPLIT),
            [HBM, VMEM] + [VMEM] * n_tgt,
            [VMEM] * CORE_SPLIT,
            [pltpu.VMEM((2, rows, GROUP // parts), F32)] + narrow(parts, 2),
            [
                local_bits, store["blocks", 4], store["piece", index, 0],
                *(store["moved", index, offset] for offset in range(1, n_tgt)),
            ],
        )
        store["core", index] = [partner_2(piece, "tgt", 1) for piece in store["mid", index]]

    def step_e(index):
        group, part, parts = chunks[index]
        final = index == len(chunks) - 1
        earlier = [store["out", index - 1]] if part else []
        if final:
            earlier += [store["out", chunks.index((at, count - 1, count))] for at, count in enumerate(CUTS[:-1])]
        store["out", index] = run(
            functools.partial(last_kernel, parts, part, len(CUTS) - 1 if final else 0, "tgt", 0, 0, 3),
            [shape((nodes, rank, columns) if final else (rows, GROUP), F32)],
            [HBM, VMEM] + [VMEM] * (2 * CORE_SPLIT + len(earlier)),
            [HBM if final else VMEM],
            narrow(parts, 1) + [pltpu.VMEM((rows, GROUP), F32), pltpu.SemaphoreType.DMA((len(CUTS),))],
            [local_bits, store["blocks", 6], *store["mid", index], *store["core", index], *earlier],
        )[0]

    steps = {
        "A": step_a, "P": step_p, "Q": step_q, "R": step_r,
        "B": step_b, "C": step_c, "T": step_t, "X": step_x, "S": step_s, "D": step_d, "E": step_e,
    }

    for name in ORDER:
        steps[name[0]](int(name[1:]))
    return store["out", len(chunks) - 1]


ORDER = (
    'A0',
    'A1',
    'P0',
    'Q0',
    'B0',
    'R2',
    'R3',
    'B1',
    'C0',
    'T0',
    'X0',
    'B2',
    'C1',
    'T1',
    'X1',
    'S0',
    'D0',
    'C2',
    'T2',
    'X2',
    'B3',
    'S1',
    'D1',
    'S2',
    'C3',
    'T3',
    'X3',
    'D2',
    'E0',
    'E1',
    'S3',
    'D3',
    'E2',
    'E3',
)


def solution(mesh):
    placed = (P(("src", "tgt"), None, None), P(None, ("src", "tgt"), None, None), P(), P())
    return jax.shard_map(
        on_device,
        mesh=mesh,
        in_specs=placed,
        out_specs=P(("src", "tgt"), None, None),
        check_vma=False,
    )
```
